32 devices in a mesh: group: 2 (over y), gx: 4 (over z), gz: 2 (over x), col: 2 (over core).
Axes of the slice: x: 2, y: 2, z: 4, core: 2. Of those that a mesh axis runs over, the one named last changes fastest.
Arguments:
- features: bfloat16 [32, 64, 16, 256], P(None, 'col', ('group', 'gx'), 'gz'), parts along dimension 2, may hold values from -6 to 6
- labels: int32 [64, 16, 256], P(None, ('group', 'gx'), 'gz'), parts along dimension 1, may hold values from 0 to 3
- grid_index: int32 [64], replicated, may hold values from 0 to 15
- stretch: float32 [16, 9], replicated, may hold values from 0.5 to 2
- tile_filter: float32 [32, 25], replicated, may hold values from -1.25 to 1.25
- wall_filter: float32 [32, 9], replicated, may hold values from -2 to 2
- class_weight: float32 [4, 32], replicated, may hold values from -1 to 1
Outputs:
- grad_features: bfloat16 [32, 64, 16, 256], P(None, 'col', ('group', 'gx'), 'gz'), parts along dimension 2
- grad_tile_filter: float32 [64, 25], P('group'), parts along dimension 0
- grad_wall_filter: float32 [64, 9], P('group'), parts along dimension 0
- grad_class_weight: float32 [8, 32], P('group'), parts along dimension 0
The draws below stay inside these ranges and needn't reach their ends.
There are 2 independent parts, one for each index of `group`. The reference program is written for one: setup_inputs(seed, part) draws one part's arguments, and reference() takes and returns one part's arrays. A program takes and returns all parts, laid end to end along the dimension named above; an argument that names none is the same for every part. Nothing has to cross between parts.
All inputs are finite; a program needn't handle non-finite values.
Results may differ from the reference program's by a relative error of at most 0.0064.
Values may be sent and summed in bfloat16 or wider, within the bound.
A program may use at most 64 MiB of HBM per device.

```python
import math
import jax
import jax.numpy as jnp
from jax import lax

C = 32
K = 4
L = 16
NY = 64
NX = 8
NZ = 256


def with_ends(entries, own_key, low, largest):
    longest = entries.shape.index(max(entries.shape))
    spots = []
    for shift in (0, 1):
        where = [jax.random.randint(jax.random.fold_in(own_key, axis), (), 0, length) for axis, length in enumerate(entries.shape)]
        where[longest] = (where[longest] + shift) % entries.shape[longest]
        spots.append(tuple(where))
    return entries.at[spots[0]].set(low).at[spots[1]].set(largest)


def block_levels(own_key, shape, shards, low, high):
    loudness, own = 1.0, jax.random.fold_in(own_key, 6)
    for position, parts in shards:
        draws = jnp.exp(jax.random.uniform(jax.random.fold_in(own, position), (parts,), jnp.float32, low / len(shards), high / len(shards)))
        loudness = loudness * jnp.repeat(draws, shape[position] // parts).reshape([-1 if axis == position else 1 for axis in range(len(shape))])
    return loudness


def centred(stream_key, shape, deviation, reach, cuts=(), kind=jnp.bfloat16):
    level = block_levels(stream_key, shape, cuts, -0.22, 0.18) if cuts else 1.0
    values = jax.random.normal(stream_key, shape, jnp.float32) * deviation * level
    return jnp.minimum(jnp.maximum(values, -reach), reach).astype(kind)


def setup_inputs(seed: int = 0, part: int = 0) -> dict:
    splits = jax.random.split(jax.random.key(seed), 8)
    part_splits = jax.random.split(jax.random.fold_in(splits[7], part), 8)
    features = centred(part_splits[0], (C, NY, NX, NZ), 1.0, 6.0, ((1, 2), (2, 4), (3, 2)))
    labels = with_ends(jax.random.randint(part_splits[1], (NY, NX, NZ), 0, K), jax.random.fold_in(part_splits[1], 1), 0, K - 1).astype(jnp.int32)
    grid_index = with_ends(jax.random.randint(splits[2], (NY,), 0, L), jax.random.fold_in(splits[2], 1), 0, L - 1).astype(jnp.int32)
    stretch = jnp.clip(jnp.exp(jax.random.uniform(splits[3], (L, 9), jnp.float32, math.log(0.5), math.log(2.0))), 0.5, 2.0)
    tile_filter = centred(splits[4], (C, 25), 25 ** -0.5, 1.25, (), jnp.float32)
    wall_filter = centred(splits[5], (C, 9), 9 ** -0.5, 2.0, (), jnp.float32)
    class_weight = centred(splits[6], (K, C), C ** -0.5, 1.0, (), jnp.float32)
    return dict(features=features, labels=labels, grid_index=grid_index, stretch=stretch, tile_filter=tile_filter, wall_filter=wall_filter, class_weight=class_weight)


def band_table(grid_index, stretch):
    levels = stretch.shape[0]
    onehot = (grid_index[:, None] == jnp.arange(levels, dtype=jnp.int32)[None, :]).astype(jnp.float32)
    return jnp.dot(onehot, stretch, precision=lax.Precision.HIGHEST)


def channel_forward(field, tile_row, wall_row, bands):
    rows = field.shape[0]
    values = field.astype(jnp.float32)
    smooth = jnp.zeros(values.shape, jnp.float32)
    for i in range(5):
        for j in range(5):
            smooth = smooth + tile_row[5 * i + j] * jnp.roll(values, (2 - i, 2 - j), axis=(1, 2))
    smoothed = smooth.astype(jnp.bfloat16)
    padded = jnp.pad(smoothed.astype(jnp.float32), ((4, 4), (0, 0), (0, 0)))
    wall_out = jnp.zeros(values.shape, jnp.float32)
    for k in range(9):
        tap = wall_row[k] * bands[:, k]
        wall_out = wall_out + tap[:, None, None] * padded[k:k + rows]
    return values, padded, wall_out


def reference(features, labels, grid_index, stretch, tile_filter, wall_filter, class_weight):
    classes = class_weight.shape[0]
    rows = features.shape[1]
    volume = features.shape[1] * features.shape[2] * features.shape[3]
    bands = band_table(grid_index, stretch)
    bands_pad = jnp.pad(bands, ((4, 4), (0, 0)))

    def forward_step(total, items):
        field, tile_row, wall_row, class_col = items
        values, padded, wall_out = channel_forward(field, tile_row, wall_row, bands)
        hidden = wall_out * jax.nn.sigmoid(wall_out)
        return total + class_col[:, None, None, None] * hidden[None], None

    start = jnp.zeros((classes,) + features.shape[1:], jnp.float32)
    scores, unused = lax.scan(forward_step, start, (features, tile_filter, wall_filter, class_weight.T))
    targets = (labels[None] == jnp.arange(classes, dtype=jnp.int32)[:, None, None, None]).astype(jnp.float32)
    errors = scores - targets

    def backward_step(carry, items):
        field, tile_row, wall_row, class_col = items
        values, padded, wall_out = channel_forward(field, tile_row, wall_row, bands)
        sig = jax.nn.sigmoid(wall_out)
        hidden = wall_out * sig
        grad_hidden = jnp.einsum('k,kyxz->yxz', class_col, errors, precision=lax.Precision.HIGHEST)
        grad_wall = (grad_hidden * sig * (1.0 + wall_out * (1.0 - sig))).astype(jnp.bfloat16)
        class_grad = jnp.einsum('kyxz,yxz->k', errors, hidden, precision=lax.Precision.HIGHEST)
        wall_vals = grad_wall.astype(jnp.float32)
        wall_grad = jnp.stack([jnp.sum(wall_vals * bands[:, k][:, None, None] * padded[k:k + rows]) for k in range(9)])
        wall_pad = jnp.pad(wall_vals, ((4, 4), (0, 0), (0, 0)))
        back = jnp.zeros(values.shape, jnp.float32)
        for k in range(9):
            first = 8 - k
            tap = wall_row[k] * bands_pad[first:first + rows, k]
            back = back + tap[:, None, None] * wall_pad[first:first + rows]
        grad_smooth = back.astype(jnp.bfloat16).astype(jnp.float32)
        grad_field = jnp.zeros(values.shape, jnp.float32)
        tile_grad = []
        for i in range(5):
            for j in range(5):
                grad_field = grad_field + tile_row[5 * i + j] * jnp.roll(grad_smooth, (i - 2, j - 2), axis=(1, 2))
                tile_grad.append(jnp.sum(jnp.roll(values, (2 - i, 2 - j), axis=(1, 2)) * grad_smooth))
        return carry, (grad_field.astype(jnp.bfloat16), jnp.stack(tile_grad), wall_grad, class_grad)

    unused, outs = lax.scan(backward_step, jnp.zeros((), jnp.float32), (features, tile_filter, wall_filter, class_weight.T))
    grad_features, tile_grads, wall_grads, class_grads = outs
    return grad_features, tile_grads / volume, wall_grads / volume, class_grads.T / volume
```

```python
import functools

import jax
import jax.numpy as jnp
from jax import lax
from jax.experimental import pallas as pl
from jax.experimental.pallas import tpu as pltpu
from jax.sharding import PartitionSpec as P

F32 = jnp.float32
BF16 = jnp.bfloat16
MESH = pl.DeviceIdType.MESH


def fold(value):
    total = value[0:8]
    for row in range(8, value.shape[0], 8):
        total = total + value[row : row + 8]
    return total


def rounded(value):
    return value.astype(BF16).astype(F32)


def kernel(
    dims,
    feat, labels, bands, tile_w, wall_w, class_w,
    out, small,
    recv, halo_out, halo_in, zfeat, smooth, stage, taps, band_rows, hid, slope,
    part_own, part_out, part_in, err, gwall, gsm, ghalo_out, ghalo_in, zgrad, gout, gstage,
    acc, red, sums,
    a_send, a_recv, own_sem, h_send, h_recv, s_send, s_recv, p_send, p_recv, e_send, e_recv,
    w_send, w_recv, g_send, g_recv, o_send, o_recv, r_send, r_recv,
):
    size, depth, cpg, chunks = dims
    per = cpg // chunks
    xs = 2 * size
    xgroups = xs // 8
    everyone = size * depth * 2
    gx, gz, col = lax.axis_index("gx"), lax.axis_index("gz"), lax.axis_index("col")
    me = (gx * depth + gz) * 2 + col
    other = 1 - col
    right, left = lax.rem(gz + 1, depth), lax.rem(gz + depth - 1, depth)
    chan0 = gx * cpg

    def peer(step):
        return lax.rem(gx + step, size)

    def source(step):
        return lax.rem(gx + size - step, size)

    def coords(step):
        index = lax.rem(me + step, everyone)
        return {
            "gx": index // (2 * depth),
            "gz": lax.rem(index // 2, depth),
            "col": lax.rem(index, 2),
        }

    barrier = pltpu.get_barrier_semaphore()

    @pl.loop(1, everyone)
    def _(step):
        pl.semaphore_signal(barrier, inc=1, device_id=coords(step), device_id_type=MESH)

    pl.semaphore_wait(barrier, everyone - 1)

    def remote(src, dst, send, rec, device):
        return pltpu.make_async_remote_copy(
            src_ref=src, dst_ref=dst, send_sem=send, recv_sem=rec,
            device_id=device, device_id_type=MESH,
        )

    def a_copy(chunk, step):
        return remote(
            feat.at[pl.ds(peer(step) * cpg + chunk * per, per)],
            recv.at[step, pl.ds(chunk * per, per)],
            a_send.at[chunk, step], a_recv.at[chunk, step], {"gx": peer(step)},
        )

    def h_copy(way, step):
        return remote(
            halo_out.at[peer(step)], halo_in.at[way, step],
            h_send.at[way, step], h_recv.at[way, step],
            {"gx": peer(step), "gz": right if way == 0 else left},
        )

    own_copy = pltpu.make_async_copy(feat.at[pl.ds(chan0, cpg)], recv.at[0], own_sem)
    own_copy.start()
    for step in range(1, size):
        a_copy(0, step).start()

    lane = lax.broadcasted_iota(jnp.int32, (8, 128), 1)
    quad = lane // 4

    @pl.loop(0, size)
    def _(group):
        for first in range(0, cpg, 4):
            packed = jnp.zeros((8, 128), F32)
            for c in range(first, min(first + 4, cpg)):
                stage[c] = feat[group * cpg + c].astype(F32)
                for xl in range(2):
                    rows = stage[c, pl.ds(xl, 32, stride=2), :]
                    for t in range(4):
                        m = (c - first) * 8 + xl * 4 + t
                        turned = pltpu.roll(rows[8 * t : 8 * t + 8], (2 + 4 * m) % 128, 1)
                        packed = jnp.where(quad == m, turned, packed)
            halo_out[group, pl.ds(first // 4 * 8, 8), :] = packed

    for way in range(2):
        for step in range(size):
            h_copy(way, step).start()
    for chunk in range(1, chunks):
        for step in range(1, size):
            a_copy(chunk, step).start()

    for k in range(9):
        band_rows[k] = jnp.broadcast_to(bands[pl.ds(32 * col, 48), k : k + 1], (48, 128))

    @pl.loop(0, cpg)
    def _(c):
        for k in range(9):
            taps[c, k] = wall_w[chan0 + c, k] * band_rows[k]
        for x_group in range(0, xs, 8):
            blank = jnp.zeros((8, 8, 128), F32)
            smooth[c, pl.ds(x_group, 8), pl.ds(pl.multiple_of(40 * col, 8), 8), :] = blank
            gwall[c, pl.ds(x_group, 8), pl.ds(pl.multiple_of(40 * col, 8), 8), :] = blank
        for q in range(40):
            acc[c, q] = jnp.zeros((8, 128), F32)

    red[...] = jnp.zeros((128, 128), F32)

    def shifts(value, edge):
        return (
            pltpu.roll(jnp.where(lane >= 126, edge, value), 2, 1),
            pltpu.roll(jnp.where(lane == 127, edge, value), 1, 1),
            value,
            pltpu.roll(jnp.where(lane == 0, edge, value), 127, 1),
            pltpu.roll(jnp.where(lane < 2, edge, value), 126, 1),
        )

    def filtered(field, c, x, flip):
        total = None
        for i in range(5):
            at = lax.rem(x + (4 - i if flip else i) - 2 + xs, xs)
            for j in range(5):
                term = tile_w[chan0 + c, 5 * i + j] * field[4 - j if flip else j, c, at]
                total = term if total is None else total + term
        return total

    def y_copy(ref, index, send, rec):
        src = pl.multiple_of(32 - 24 * col, 8)
        dst = pl.multiple_of(40 * col, 8)
        return remote(
            ref.at[index + (pl.ds(src, 8),)], ref.at[index + (pl.ds(dst, 8),)],
            send, rec, {"col": other},
        )

    def s_copy(c):
        return y_copy(smooth, (c, pl.ds(0, xs)), s_send.at[c], s_recv.at[c])

    own_copy.wait()
    for way in range(2):
        for step in range(size):
            h_copy(way, step).wait_recv()

    def edges_of(ref_left, ref_right):
        return jnp.where(lax.rem(lane, 4) < 2, ref_left, ref_right)

    for chunk in range(chunks):
        for step in range(1, size):
            a_copy(chunk, step).wait_recv()
        for c in range(chunk * per, chunk * per + per):

            @pl.loop(0, size)
            def _(step, c=c):
                s = source(step)
                stage[step] = recv[step, c].astype(F32)
                at = pl.ds(c // 4 * 8, 8)
                packed = edges_of(halo_in[0, step, at, :], halo_in[1, step, at, :])
                for xl in range(2):
                    rows = stage[step, pl.ds(xl, 32, stride=2), :]
                    for t in range(4):
                        m = c % 4 * 8 + xl * 4 + t
                        edge = pltpu.roll(packed, (126 - 4 * m) % 128, 1)
                        moved = shifts(rows[8 * t : 8 * t + 8], edge)
                        for j in range(5):
                            zfeat[j, c, 2 * s + xl, pl.ds(8 * t, 8), :] = moved[j]

            @pl.loop(0, xs)
            def _(x, c=c):
                smooth[c, x, pl.ds(8, 32), :] = rounded(filtered(zfeat, c, x, False))

            s_copy(c).start()

    for c in range(cpg):
        s_copy(c).wait_recv()

    def p_copy(step):
        return remote(
            part_out.at[step], part_in.at[step], p_send.at[step], p_recv.at[step],
            {"gx": peer(step)},
        )

    def scores_at(x):
        def body(c, totals):
            wall = None
            for k in range(9):
                term = taps[c, k, pl.ds(8, 32), :] * smooth[c, x, pl.ds(4 + k, 32), :]
                wall = term if wall is None else wall + term
            sig = jax.nn.sigmoid(wall)
            hidden = wall * sig
            hid[c, x] = hidden
            slope[c, x] = sig * (1.0 + wall * (1.0 - sig))
            return tuple(
                total + class_w[k, chan0 + c] * hidden for k, total in enumerate(totals)
            )

        return lax.fori_loop(0, cpg, body, tuple(jnp.zeros((32, 128), F32) for k in range(4)))

    @pl.loop(1, size)
    def _(step):
        for xl in range(2):
            totals = scores_at(2 * peer(step) + xl)
            for k in range(4):
                part_out[step, pl.ds((2 * k + xl) * 32, 32), :] = totals[k].astype(BF16)
        p_copy(step).start()

    for xl in range(2):
        totals = scores_at(2 * gx + xl)
        for k in range(4):
            part_own[pl.ds((2 * k + xl) * 32, 32), :] = totals[k]

    @pl.loop(1, size)
    def _(step):
        p_copy(step).wait_recv()
        part_own[...] = part_own[...] + part_in[step].astype(F32)

    for xl in range(2):
        marks = labels[pl.ds(64 * col + xl, 32, stride=2), :]
        for k in range(4):
            at = pl.ds((2 * k + xl) * 32, 32)
            err[0, at, :] = (part_own[at, :] - jnp.where(marks == k, 1.0, 0.0)).astype(BF16)

    def e_copy(step):
        return remote(
            err.at[0], err.at[step], e_send.at[step], e_recv.at[step], {"gx": peer(step)}
        )

    for step in range(1, size):
        e_copy(step).start()

    def w_copy(step):
        return y_copy(
            gwall, (pl.ds(0, cpg), pl.ds(2 * source(step), 2)), w_send.at[step], w_recv.at[step]
        )

    def wall_grads(step):
        for xl in range(2):
            x = 2 * source(step) + xl
            errors = [err[step, pl.ds((2 * k + xl) * 32, 32), :].astype(F32) for k in range(4)]

            @pl.loop(0, cpg)
            def _(c):
                hidden = hid[c, x]
                grad = None
                for k in range(4):
                    term = class_w[k, chan0 + c] * errors[k]
                    grad = term if grad is None else grad + term
                    acc[c, 34 + k] = acc[c, 34 + k] + fold(errors[k] * hidden)
                gwall[c, x, pl.ds(8, 32), :] = rounded(grad * slope[c, x])

        w_copy(step).start()

    wall_grads(0)

    @pl.loop(1, size)
    def _(step):
        e_copy(step).wait_recv()
        wall_grads(step)

    @pl.loop(0, size)
    def _(step):
        w_copy(step).wait_recv()

    def g_copy(way, c):
        return remote(
            ghalo_out.at[c], ghalo_in.at[way, c], g_send.at[way, c], g_recv.at[way, c],
            {"gz": right if way == 0 else left},
        )

    @pl.loop(0, cpg)
    def _(c):
        def body(x, sums9):
            grad = gwall[c, x, pl.ds(8, 32), :]
            total = None
            news = []
            for k in range(9):
                term = taps[c, k, pl.ds(12 - k, 32), :] * gwall[c, x, pl.ds(12 - k, 32), :]
                total = term if total is None else total + term
                product = grad * band_rows[k, pl.ds(8, 32), :] * smooth[c, x, pl.ds(4 + k, 32), :]
                news.append(sums9[k] + fold(product))
            gsm[c, x] = rounded(total)
            return tuple(news)

        sums9 = lax.fori_loop(0, xs, body, tuple(jnp.zeros((8, 128), F32) for k in range(9)))
        for k in range(9):
            acc[c, 25 + k] = sums9[k]

        @pl.loop(0, xgroups)
        def _(group):
            packed = jnp.zeros((8, 128), F32)
            for m in range(32):
                piece = gsm[c, group * 8 + m // 4, pl.ds(m % 4 * 8, 8), :]
                packed = jnp.where(quad == m, pltpu.roll(piece, (2 + 4 * m) % 128, 1), packed)
            ghalo_out[c, group] = packed

        for way in range(2):
            g_copy(way, c).start()

    def o_copy(chunk, step):
        return remote(
            gout.at[peer(step), pl.ds(chunk * per, per)],
            out.at[pl.ds(chan0 + chunk * per, per)],
            o_send.at[chunk, step], o_recv.at[chunk, step], {"gx": peer(step)},
        )

    @pl.loop(0, chunks)
    def _(chunk):
        @pl.loop(0, per)
        def _(lower):
            c = chunk * per + lower
            for way in range(2):
                g_copy(way, c).wait_recv()

            @pl.loop(0, xgroups)
            def _(group):
                packed = edges_of(ghalo_in[0, c, group], ghalo_in[1, c, group])
                for m in range(32):
                    at = pl.ds(m % 4 * 8, 8)
                    x = group * 8 + m // 4
                    edge = pltpu.roll(packed, (126 - 4 * m) % 128, 1)
                    moved = shifts(gsm[c, x, at, :], edge)
                    for j in range(5):
                        zgrad[j, c, x, at, :] = moved[j]

            @pl.loop(0, size)
            def _(s):
                for xl in range(2):
                    gstage[s, pl.ds(xl, 32, stride=2), :] = filtered(zgrad, c, 2 * s + xl, True)
                gout[s, c] = gstage[s].astype(BF16)

            out[chan0 + c] = gout[gx, c]

        for step in range(1, size):
            o_copy(chunk, step).start()

    row = lax.broadcasted_iota(jnp.int32, (8, 128), 0)

    @pl.loop(0, cpg)
    def _(c):
        def body(x, sums25):
            grad = gsm[c, x]
            news = []
            for i in range(5):
                at = lax.rem(x + i - 2 + xs, xs)
                for j in range(5):
                    news.append(sums25[5 * i + j] + fold(zfeat[j, c, at] * grad))
            return tuple(news)

        sums25 = lax.fori_loop(0, xs, body, tuple(jnp.zeros((8, 128), F32) for q in range(25)))
        for q in range(38):
            value = sums25[q] if q < 25 else acc[c, q]
            red[pl.ds(q, 1), :] = jnp.sum(value, axis=0, keepdims=True)
        line = lax.dot_general(
            jnp.ones((8, 128), F32), red[...], (((1,), (1,)), ((), ())),
            precision=lax.Precision.HIGHEST, preferred_element_type=F32,
        )
        before = jnp.where(c == 0, jnp.zeros((8, 128), F32), sums[me])
        sums[me] = jnp.where(row == c, line, before)

    def r_copy(step):
        return remote(sums.at[me], sums.at[me], r_send.at[step], r_recv.at[step], coords(step))

    @pl.loop(1, everyone)
    def _(step):
        r_copy(step).start()

    @pl.loop(1, everyone)
    def _(step):
        r_copy(step).wait_recv()

    @pl.loop(0, size)
    def _(group):
        total = sums[group * depth * 2]
        for member in range(1, depth * 2):
            total = total + sums[group * depth * 2 + member]
        small[group] = total

    for chunk in range(chunks):
        for step in range(1, size):
            o_copy(chunk, step).wait()
            a_copy(chunk, step).wait_send()
    for way in range(2):
        for step in range(size):
            h_copy(way, step).wait_send()
        for c in range(cpg):
            g_copy(way, c).wait_send()
    for c in range(cpg):
        s_copy(c).wait_send()
    for step in range(1, size):
        p_copy(step).wait_send()
        e_copy(step).wait_send()
    for step in range(size):
        w_copy(step).wait_send()

    @pl.loop(1, everyone)
    def _(step):
        r_copy(step).wait_send()


def shards(features, labels, grid_index, stretch, tile_filter, wall_filter, class_weight):
    chans, rows, cells_x, cells_z = features.shape
    size, depth = lax.axis_size("gx"), lax.axis_size("gz")
    volume = labels.shape[0] * cells_x * size * cells_z * depth
    cpg = chans // size
    chunks = min(4, cpg)
    per_dest = max(cpg // 4, 1) * 8
    xs = 2 * size
    everyone = size * depth * 2
    padded = jnp.pad(grid_index, (8, 8), constant_values=-1)
    onehot = (padded[:, None] == jnp.arange(stretch.shape[0], dtype=jnp.int32)).astype(F32)
    bands = jnp.dot(onehot, stretch, precision=lax.Precision.HIGHEST)
    dma = pltpu.SemaphoreType.DMA
    vmem = pl.BlockSpec(memory_space=pltpu.VMEM)
    smem = pl.BlockSpec(memory_space=pltpu.SMEM)
    grad, small = pl.pallas_call(
        functools.partial(kernel, (size, depth, cpg, chunks)),
        out_shape=(
            jax.ShapeDtypeStruct((chans, 64, 128), BF16),
            jax.ShapeDtypeStruct((size, 8, 128), F32),
        ),
        in_specs=[vmem, vmem, vmem, smem, smem, smem],
        out_specs=(vmem, vmem),
        scratch_shapes=[
            pltpu.VMEM((size, cpg, 64, 128), BF16),
            pltpu.VMEM((size, per_dest, 128), F32),
            pltpu.VMEM((2, size, per_dest, 128), F32),
            pltpu.VMEM((5, cpg, xs, 32, 128), F32),
            pltpu.VMEM((cpg, xs, 48, 128), F32),
            pltpu.VMEM((max(cpg, size), 64, 128), F32),
            pltpu.VMEM((cpg, 9, 48, 128), F32),
            pltpu.VMEM((9, 48, 128), F32),
            pltpu.VMEM((cpg, xs, 32, 128), F32),
            pltpu.VMEM((cpg, xs, 32, 128), F32),
            pltpu.VMEM((256, 128), F32),
            pltpu.VMEM((size, 256, 128), BF16),
            pltpu.VMEM((size, 256, 128), BF16),
            pltpu.VMEM((size, 256, 128), BF16),
            pltpu.VMEM((cpg, xs, 48, 128), F32),
            pltpu.VMEM((cpg, xs, 32, 128), F32),
            pltpu.VMEM((cpg, xs // 8, 8, 128), F32),
            pltpu.VMEM((2, cpg, xs // 8, 8, 128), F32),
            pltpu.VMEM((5, cpg, xs, 32, 128), F32),
            pltpu.VMEM((size, cpg, 64, 128), BF16),
            pltpu.VMEM((size, 64, 128), F32),
            pltpu.VMEM((cpg, 40, 8, 128), F32),
            pltpu.VMEM((128, 128), F32),
            pltpu.VMEM((everyone, 8, 128), F32),
            dma((chunks, size)), dma((chunks, size)), dma(()),
            dma((2, size)), dma((2, size)),
            dma((cpg,)), dma((cpg,)),
            dma((size,)), dma((size,)),
            dma((size,)), dma((size,)),
            dma((size,)), dma((size,)),
            dma((2, cpg)), dma((2, cpg)),
            dma((chunks, size)), dma((chunks, size)),
            dma((everyone,)), dma((everyone,)),
        ],
        compiler_params=pltpu.CompilerParams(
            collective_id=0, has_side_effects=True, vmem_limit_bytes=48 * 1024 * 1024
        ),
    )(
        features.reshape(chans, 64, 128), labels.reshape(128, 128), bands,
        tile_filter, wall_filter, class_weight,
    )
    table = small[:, :cpg].reshape(chans, 128) / volume
    return (
        grad.reshape(features.shape),
        table[:, :25],
        table[:, 25:34],
        table[:, 34:38].T,
    )


def solution(mesh):
    return jax.shard_map(
        shards,
        mesh=mesh,
        in_specs=(
            P(None, "col", ("group", "gx"), "gz"),
            P(None, ("group", "gx"), "gz"),
            P(),
            P(),
            P(),
            P(),
            P(),
        ),
        out_specs=(
            P(None, "col", ("group", "gx"), "gz"),
            P("group", None),
            P("group", None),
            P("group", None),
        ),
        check_vma=False,
    )
```

```python
import functools

import jax
import jax.numpy as jnp
from jax import lax
from jax.experimental import pallas as pl
from jax.experimental.pallas import tpu as pltpu
from jax.sharding import PartitionSpec as P

F32 = jnp.float32
BF16 = jnp.bfloat16
MESH = pl.DeviceIdType.MESH


def fold(value):
    total = value[0:8]
    for row in range(8, value.shape[0], 8):
        total = total + value[row : row + 8]
    return total


def rounded(value):
    return value.astype(BF16).astype(F32)


def kernel(
    dims,
    feat, labels, bands, tile_w, wall_w, class_w,
    out, tile_out, wall_out, class_out,
    recv, band_pad, halo_out, halo_in, zfeat, smooth, stage, taps, band_rows, hid, slope,
    part_own, part_out, part_in, err, gwall, gsm, ghalo_out, ghalo_in, zgrad, gout, gstage,
    acc, red, sums,
    a_send, a_recv, own_sem, h_send, h_recv, s_send, s_recv, p_send, p_recv, e_send, e_recv,
    w_send, w_recv, g_send, g_recv, o_send, o_recv, r_send, r_recv,
):
    size, depth, cpg, chunks, volume = dims
    per = cpg // chunks
    xs = 2 * size
    xgroups = xs // 8
    everyone = size * depth * 2
    gx, gz, col = lax.axis_index("gx"), lax.axis_index("gz"), lax.axis_index("col")
    me = (gx * depth + gz) * 2 + col
    other = 1 - col
    right, left = lax.rem(gz + 1, depth), lax.rem(gz + depth - 1, depth)
    chan0 = gx * cpg

    def peer(step):
        return lax.rem(gx + step, size)

    def source(step):
        return lax.rem(gx + size - step, size)

    def coords(step):
        index = lax.rem(me + step, everyone)
        return {
            "gx": index // (2 * depth),
            "gz": lax.rem(index // 2, depth),
            "col": lax.rem(index, 2),
        }

    barrier = pltpu.get_barrier_semaphore()

    @pl.loop(1, everyone)
    def _(step):
        pl.semaphore_signal(barrier, inc=1, device_id=coords(step), device_id_type=MESH)

    pl.semaphore_wait(barrier, everyone - 1)

    def remote(src, dst, send, rec, device):
        return pltpu.make_async_remote_copy(
            src_ref=src, dst_ref=dst, send_sem=send, recv_sem=rec,
            device_id=device, device_id_type=MESH,
        )

    def a_copy(chunk, step):
        return remote(
            feat.at[pl.ds(peer(step) * cpg + chunk * per, per)],
            recv.at[step, pl.ds(chunk * per, per)],
            a_send.at[chunk, step], a_recv.at[chunk, step], {"gx": peer(step)},
        )

    def h_copy(way, step):
        return remote(
            halo_out.at[peer(step)], halo_in.at[way, step],
            h_send.at[way, step], h_recv.at[way, step],
            {"gx": peer(step), "gz": right if way == 0 else left},
        )

    own_copy = pltpu.make_async_copy(feat.at[pl.ds(chan0, cpg)], recv.at[0], own_sem)
    own_copy.start()
    for step in range(1, size):
        a_copy(0, step).start()

    lane = lax.broadcasted_iota(jnp.int32, (8, 128), 1)
    quad = lane // 4

    @pl.loop(0, size)
    def _(group):
        for first in range(0, cpg, 4):
            packed = jnp.zeros((8, 128), F32)
            for c in range(first, min(first + 4, cpg)):
                stage[c] = feat[group * cpg + c].astype(F32)
                for xl in range(2):
                    rows = stage[c, pl.ds(xl, 32, stride=2), :]
                    for t in range(4):
                        m = (c - first) * 8 + xl * 4 + t
                        turned = pltpu.roll(rows[8 * t : 8 * t + 8], (2 + 4 * m) % 128, 1)
                        packed = jnp.where(quad == m, turned, packed)
            halo_out[group, pl.ds(first // 4 * 8, 8), :] = packed

    for way in range(2):
        for step in range(size):
            h_copy(way, step).start()
    for chunk in range(1, chunks):
        for step in range(1, size):
            a_copy(chunk, step).start()

    band_pad[0:8] = jnp.zeros((8, 9), F32)
    band_pad[8:72] = bands[...]
    band_pad[72:80] = jnp.zeros((8, 9), F32)
    for k in range(9):
        band_rows[k] = jnp.broadcast_to(band_pad[pl.ds(32 * col, 48), k : k + 1], (48, 128))

    @pl.loop(0, cpg)
    def _(c):
        for k in range(9):
            taps[c, k] = wall_w[k, chan0 + c] * band_rows[k]
        for x_group in range(0, xs, 8):
            blank = jnp.zeros((8, 8, 128), F32)
            smooth[c, pl.ds(x_group, 8), pl.ds(pl.multiple_of(40 * col, 8), 8), :] = blank
            gwall[c, pl.ds(x_group, 8), pl.ds(pl.multiple_of(40 * col, 8), 8), :] = blank
        for q in range(40):
            acc[c, q] = jnp.zeros((8, 128), F32)

    red[...] = jnp.zeros((128, 128), F32)

    def shifts(value, edge):
        return (
            pltpu.roll(jnp.where(lane >= 126, edge, value), 2, 1),
            pltpu.roll(jnp.where(lane == 127, edge, value), 1, 1),
            value,
            pltpu.roll(jnp.where(lane == 0, edge, value), 127, 1),
            pltpu.roll(jnp.where(lane < 2, edge, value), 126, 1),
        )

    def filtered(field, c, x, flip):
        total = None
        for i in range(5):
            at = lax.rem(x + (4 - i if flip else i) - 2 + xs, xs)
            for j in range(5):
                term = tile_w[chan0 + c, 5 * i + j] * field[4 - j if flip else j, c, at]
                total = term if total is None else total + term
        return total

    def y_copy(ref, index, send, rec):
        src = pl.multiple_of(32 - 24 * col, 8)
        dst = pl.multiple_of(40 * col, 8)
        return remote(
            ref.at[index + (pl.ds(src, 8),)], ref.at[index + (pl.ds(dst, 8),)],
            send, rec, {"col": other},
        )

    def s_copy(c):
        return y_copy(smooth, (c, pl.ds(0, xs)), s_send.at[c], s_recv.at[c])

    own_copy.wait()
    for way in range(2):
        for step in range(size):
            h_copy(way, step).wait_recv()

    def edges_of(ref_left, ref_right):
        return jnp.where(lax.rem(lane, 4) < 2, ref_left, ref_right)

    for chunk in range(chunks):
        for step in range(1, size):
            a_copy(chunk, step).wait_recv()
        for c in range(chunk * per, chunk * per + per):

            @pl.loop(0, size, unroll=2)
            def _(step, c=c):
                s = source(step)
                stage[step] = recv[step, c].astype(F32)
                at = pl.ds(c // 4 * 8, 8)
                packed = edges_of(halo_in[0, step, at, :], halo_in[1, step, at, :])
                for xl in range(2):
                    rows = stage[step, pl.ds(xl, 32, stride=2), :]
                    for t in range(4):
                        m = c % 4 * 8 + xl * 4 + t
                        edge = pltpu.roll(packed, (126 - 4 * m) % 128, 1)
                        moved = shifts(rows[8 * t : 8 * t + 8], edge)
                        for j in range(5):
                            zfeat[j, c, 2 * s + xl, pl.ds(8 * t, 8), :] = moved[j]

            @pl.loop(0, xs, unroll=4)
            def _(x, c=c):
                smooth[c, x, pl.ds(8, 32), :] = rounded(filtered(zfeat, c, x, False))

            s_copy(c).start()

    for c in range(cpg):
        s_copy(c).wait_recv()

    def p_copy(step):
        return remote(
            part_out.at[step], part_in.at[step], p_send.at[step], p_recv.at[step],
            {"gx": peer(step)},
        )

    def scores_at(x):
        def body(c, totals):
            wall = None
            for k in range(9):
                term = taps[c, k, pl.ds(8, 32), :] * smooth[c, x, pl.ds(4 + k, 32), :]
                wall = term if wall is None else wall + term
            sig = jax.nn.sigmoid(wall)
            hidden = wall * sig
            hid[c, x] = hidden
            slope[c, x] = sig * (1.0 + wall * (1.0 - sig))
            return tuple(
                total + class_w[k, chan0 + c] * hidden for k, total in enumerate(totals)
            )

        return lax.fori_loop(
            0, cpg, body, tuple(jnp.zeros((32, 128), F32) for k in range(4)), unroll=min(4, cpg)
        )

    @pl.loop(1, size)
    def _(step):
        for xl in range(2):
            totals = scores_at(2 * peer(step) + xl)
            for k in range(4):
                part_out[step, pl.ds((2 * k + xl) * 32, 32), :] = totals[k].astype(BF16)
        p_copy(step).start()

    for xl in range(2):
        totals = scores_at(2 * gx + xl)
        for k in range(4):
            part_own[pl.ds((2 * k + xl) * 32, 32), :] = totals[k]

    @pl.loop(1, size)
    def _(step):
        p_copy(step).wait_recv()
        part_own[...] = part_own[...] + part_in[step].astype(F32)

    for xl in range(2):
        marks = labels[pl.ds(64 * col + xl, 32, stride=2), :]
        for k in range(4):
            at = pl.ds((2 * k + xl) * 32, 32)
            err[0, at, :] = (part_own[at, :] - jnp.where(marks == k, 1.0, 0.0)).astype(BF16)

    def e_copy(step):
        return remote(
            err.at[0], err.at[step], e_send.at[step], e_recv.at[step], {"gx": peer(step)}
        )

    for step in range(1, size):
        e_copy(step).start()

    def w_copy(step):
        return y_copy(
            gwall, (pl.ds(0, cpg), pl.ds(2 * source(step), 2)), w_send.at[step], w_recv.at[step]
        )

    def wall_grads(step):
        for xl in range(2):
            x = 2 * source(step) + xl
            errors = [err[step, pl.ds((2 * k + xl) * 32, 32), :].astype(F32) for k in range(4)]

            @pl.loop(0, cpg, unroll=min(4, cpg))
            def _(c):
                hidden = hid[c, x]
                grad = None
                for k in range(4):
                    term = class_w[k, chan0 + c] * errors[k]
                    grad = term if grad is None else grad + term
                    acc[c, 34 + k] = acc[c, 34 + k] + fold(errors[k] * hidden)
                gwall[c, x, pl.ds(8, 32), :] = rounded(grad * slope[c, x])

        w_copy(step).start()

    wall_grads(0)

    @pl.loop(1, size)
    def _(step):
        e_copy(step).wait_recv()
        wall_grads(step)

    @pl.loop(0, size)
    def _(step):
        w_copy(step).wait_recv()

    def g_copy(way, c):
        return remote(
            ghalo_out.at[c], ghalo_in.at[way, c], g_send.at[way, c], g_recv.at[way, c],
            {"gz": right if way == 0 else left},
        )

    @pl.loop(0, cpg)
    def _(c):
        def body(x, sums9):
            grad = gwall[c, x, pl.ds(8, 32), :]
            total = None
            news = []
            for k in range(9):
                term = taps[c, k, pl.ds(12 - k, 32), :] * gwall[c, x, pl.ds(12 - k, 32), :]
                total = term if total is None else total + term
                product = grad * band_rows[k, pl.ds(8, 32), :] * smooth[c, x, pl.ds(4 + k, 32), :]
                news.append(sums9[k] + fold(product))
            gsm[c, x] = rounded(total)
            return tuple(news)

        sums9 = lax.fori_loop(0, xs, body, tuple(jnp.zeros((8, 128), F32) for k in range(9)), unroll=2)
        for k in range(9):
            acc[c, 25 + k] = sums9[k]

        @pl.loop(0, xgroups)
        def _(group):
            packed = jnp.zeros((8, 128), F32)
            for m in range(32):
                piece = gsm[c, group * 8 + m // 4, pl.ds(m % 4 * 8, 8), :]
                packed = jnp.where(quad == m, pltpu.roll(piece, (2 + 4 * m) % 128, 1), packed)
            ghalo_out[c, group] = packed

        for way in range(2):
            g_copy(way, c).start()

    def o_copy(chunk, step):
        return remote(
            gout.at[peer(step), pl.ds(chunk * per, per)],
            out.at[pl.ds(chan0 + chunk * per, per)],
            o_send.at[chunk, step], o_recv.at[chunk, step], {"gx": peer(step)},
        )

    @pl.loop(0, chunks)
    def _(chunk):
        @pl.loop(0, per)
        def _(lower):
            c = chunk * per + lower
            for way in range(2):
                g_copy(way, c).wait_recv()

            @pl.loop(0, xgroups)
            def _(group):
                packed = edges_of(ghalo_in[0, c, group], ghalo_in[1, c, group])
                for m in range(32):
                    at = pl.ds(m % 4 * 8, 8)
                    x = group * 8 + m // 4
                    edge = pltpu.roll(packed, (126 - 4 * m) % 128, 1)
                    moved = shifts(gsm[c, x, at, :], edge)
                    for j in range(5):
                        zgrad[j, c, x, at, :] = moved[j]

            @pl.loop(0, size, unroll=2)
            def _(s):
                for xl in range(2):
                    gstage[s, pl.ds(xl, 32, stride=2), :] = filtered(zgrad, c, 2 * s + xl, True)
                gout[s, c] = gstage[s].astype(BF16)

            out[chan0 + c] = gout[gx, c]

        for step in range(1, size):
            o_copy(chunk, step).start()

    row = lax.broadcasted_iota(jnp.int32, (8, 128), 0)

    @pl.loop(0, cpg)
    def _(c):
        def body(x, sums25):
            grad = gsm[c, x]
            news = []
            for i in range(5):
                at = lax.rem(x + i - 2 + xs, xs)
                for j in range(5):
                    news.append(sums25[5 * i + j] + fold(zfeat[j, c, at] * grad))
            return tuple(news)

        sums25 = lax.fori_loop(0, xs, body, tuple(jnp.zeros((8, 128), F32) for q in range(25)), unroll=2)
        for q in range(38):
            value = sums25[q] if q < 25 else acc[c, q]
            red[pl.ds(q, 1), :] = jnp.sum(value, axis=0, keepdims=True)
        line = lax.dot_general(
            jnp.ones((8, 128), F32), red[...], (((1,), (1,)), ((), ())),
            precision=lax.Precision.HIGHEST, preferred_element_type=F32,
        )
        before = jnp.where(c == 0, jnp.zeros((8, 128), F32), sums[me])
        sums[me] = jnp.where(row == c, line, before)

    def r_copy(step):
        return remote(sums.at[me], sums.at[me], r_send.at[step], r_recv.at[step], coords(step))

    @pl.loop(1, everyone)
    def _(step):
        r_copy(step).start()

    @pl.loop(1, everyone)
    def _(step):
        r_copy(step).wait_recv()

    @pl.loop(0, size)
    def _(group):
        total = sums[group * depth * 2]
        for member in range(1, depth * 2):
            total = total + sums[group * depth * 2 + member]
        red[pl.ds(group * cpg, cpg), :] = total[0:cpg] / volume

    turned = red[...].T
    chans = size * cpg
    tile_out[...] = red[0:chans, 0:25]
    wall_out[...] = turned[25:34, 0:chans]
    class_out[...] = turned[34:38, 0:chans]

    for chunk in range(chunks):
        for step in range(1, size):
            o_copy(chunk, step).wait()
            a_copy(chunk, step).wait_send()
    for way in range(2):
        for step in range(size):
            h_copy(way, step).wait_send()
        for c in range(cpg):
            g_copy(way, c).wait_send()
    for c in range(cpg):
        s_copy(c).wait_send()
    for step in range(1, size):
        p_copy(step).wait_send()
        e_copy(step).wait_send()
    for step in range(size):
        w_copy(step).wait_send()

    @pl.loop(1, everyone)
    def _(step):
        r_copy(step).wait_send()


def shards(features, labels, grid_index, stretch, tile_filter, wall_filter, class_weight):
    chans, rows, cells_x, cells_z = features.shape
    size, depth = lax.axis_size("gx"), lax.axis_size("gz")
    volume = labels.shape[0] * cells_x * size * cells_z * depth
    cpg = chans // size
    chunks = min(4, cpg)
    per_dest = max(cpg // 4, 1) * 8
    xs = 2 * size
    everyone = size * depth * 2
    onehot = (grid_index[:, None] == jnp.arange(stretch.shape[0], dtype=jnp.int32)).astype(F32)
    bands = jnp.dot(onehot, stretch, precision=lax.Precision.HIGHEST)
    dma = pltpu.SemaphoreType.DMA
    vmem = pl.BlockSpec(memory_space=pltpu.VMEM)
    smem = pl.BlockSpec(memory_space=pltpu.SMEM)
    grad, tile_grad, wall_grad, class_grad = pl.pallas_call(
        functools.partial(kernel, (size, depth, cpg, chunks, volume)),
        out_shape=(
            jax.ShapeDtypeStruct((chans, 64, 128), BF16),
            jax.ShapeDtypeStruct((chans, 25), F32),
            jax.ShapeDtypeStruct((9, chans), F32),
            jax.ShapeDtypeStruct((4, chans), F32),
        ),
        in_specs=[vmem, vmem, vmem, smem, smem, smem],
        out_specs=(vmem, vmem, vmem, vmem),
        scratch_shapes=[
            pltpu.VMEM((size, cpg, 64, 128), BF16),
            pltpu.VMEM((80, 9), F32),
            pltpu.VMEM((size, per_dest, 128), F32),
            pltpu.VMEM((2, size, per_dest, 128), F32),
            pltpu.VMEM((5, cpg, xs, 32, 128), F32),
            pltpu.VMEM((cpg, xs, 48, 128), F32),
            pltpu.VMEM((max(cpg, size), 64, 128), F32),
            pltpu.VMEM((cpg, 9, 48, 128), F32),
            pltpu.VMEM((9, 48, 128), F32),
            pltpu.VMEM((cpg, xs, 32, 128), F32),
            pltpu.VMEM((cpg, xs, 32, 128), F32),
            pltpu.VMEM((256, 128), F32),
            pltpu.VMEM((size, 256, 128), BF16),
            pltpu.VMEM((size, 256, 128), BF16),
            pltpu.VMEM((size, 256, 128), BF16),
            pltpu.VMEM((cpg, xs, 48, 128), F32),
            pltpu.VMEM((cpg, xs, 32, 128), F32),
            pltpu.VMEM((cpg, xs // 8, 8, 128), F32),
            pltpu.VMEM((2, cpg, xs // 8, 8, 128), F32),
            pltpu.VMEM((5, cpg, xs, 32, 128), F32),
            pltpu.VMEM((size, cpg, 64, 128), BF16),
            pltpu.VMEM((size, 64, 128), F32),
            pltpu.VMEM((cpg, 40, 8, 128), F32),
            pltpu.VMEM((128, 128), F32),
            pltpu.VMEM((everyone, 8, 128), F32),
            dma((chunks, size)), dma((chunks, size)), dma(()),
            dma((2, size)), dma((2, size)),
            dma((cpg,)), dma((cpg,)),
            dma((size,)), dma((size,)),
            dma((size,)), dma((size,)),
            dma((size,)), dma((size,)),
            dma((2, cpg)), dma((2, cpg)),
            dma((chunks, size)), dma((chunks, size)),
            dma((everyone,)), dma((everyone,)),
        ],
        compiler_params=pltpu.CompilerParams(
            collective_id=0, has_side_effects=True, vmem_limit_bytes=48 * 1024 * 1024
        ),
    )(
        features.reshape(chans, 64, 128), labels.reshape(128, 128), bands,
        tile_filter, wall_filter.T, class_weight,
    )
    return grad.reshape(features.shape), tile_grad, wall_grad.T, class_grad


def solution(mesh):
    return jax.shard_map(
        shards,
        mesh=mesh,
        in_specs=(
            P(None, "col", ("group", "gx"), "gz"),
            P(None, ("group", "gx"), "gz"),
            P(),
            P(),
            P(),
            P(),
            P(),
        ),
        out_specs=(
            P(None, "col", ("group", "gx"), "gz"),
            P("group", None),
            P("group", None),
            P("group", None),
        ),
        check_vma=False,
    )
```

```python
import functools

import jax
import jax.numpy as jnp
from jax import lax
from jax.experimental import pallas as pl
from jax.experimental.pallas import tpu as pltpu
from jax.sharding import PartitionSpec as P

F32 = jnp.float32
BF16 = jnp.bfloat16
MESH = pl.DeviceIdType.MESH


def fold(value):
    total = value[0:8]
    for row in range(8, value.shape[0], 8):
        total = total + value[row : row + 8]
    return total


def rounded(value):
    return value.astype(BF16).astype(F32)


def kernel(
    dims,
    feat, labels, bands, tile_w, wall_w, class_w,
    out, tile_out, wall_out, class_out,
    recv, band_pad, halo_out, halo_in, zfeat, smooth, stage, taps, band_rows, hid, slope,
    part_own, part_out, part_in, err, gwall, gsm, ghalo_out, ghalo_in, zgrad, gout, gstage,
    taps_back, red, sums,
    a_send, a_recv, own_sem, h_send, h_recv, s_send, s_recv, p_send, p_recv, e_send, e_recv,
    w_send, w_recv, g_send, g_recv, o_send, o_recv, r_send, r_recv,
):
    size, depth, cpg, chunks, volume = dims
    per = cpg // chunks
    xs = 2 * size
    xgroups = xs // 8
    everyone = size * depth * 2
    gx, gz, col = lax.axis_index("gx"), lax.axis_index("gz"), lax.axis_index("col")
    me = (gx * depth + gz) * 2 + col
    other = 1 - col
    right, left = lax.rem(gz + 1, depth), lax.rem(gz + depth - 1, depth)
    chan0 = gx * cpg

    def peer(step):
        return lax.rem(gx + step, size)

    def source(step):
        return lax.rem(gx + size - step, size)

    def coords(step):
        index = lax.rem(me + step, everyone)
        return {
            "gx": index // (2 * depth),
            "gz": lax.rem(index // 2, depth),
            "col": lax.rem(index, 2),
        }

    barrier = pltpu.get_barrier_semaphore()

    @pl.loop(1, everyone)
    def _(step):
        pl.semaphore_signal(barrier, inc=1, device_id=coords(step), device_id_type=MESH)

    pl.semaphore_wait(barrier, everyone - 1)

    def remote(src, dst, send, rec, device):
        return pltpu.make_async_remote_copy(
            src_ref=src, dst_ref=dst, send_sem=send, recv_sem=rec,
            device_id=device, device_id_type=MESH,
        )

    def a_copy(chunk, step):
        return remote(
            feat.at[pl.ds(peer(step) * cpg + chunk * per, per)],
            recv.at[step, pl.ds(chunk * per, per)],
            a_send.at[chunk, step], a_recv.at[chunk, step], {"gx": peer(step)},
        )

    def h_copy(way, step):
        return remote(
            halo_out.at[peer(step)], halo_in.at[way, step],
            h_send.at[way, step], h_recv.at[way, step],
            {"gx": peer(step), "gz": right if way == 0 else left},
        )

    own_copy = pltpu.make_async_copy(feat.at[pl.ds(chan0, cpg)], recv.at[0], own_sem)
    own_copy.start()
    for step in range(1, size):
        a_copy(0, step).start()

    lane = lax.broadcasted_iota(jnp.int32, (8, 128), 1)
    quad = lane // 4

    @pl.loop(0, size)
    def _(group):
        for first in range(0, cpg, 4):
            packed = jnp.zeros((8, 128), F32)
            for c in range(first, min(first + 4, cpg)):
                stage[c] = feat[group * cpg + c].astype(F32)
                for xl in range(2):
                    rows = stage[c, pl.ds(xl, 32, stride=2), :]
                    for t in range(4):
                        m = (c - first) * 8 + xl * 4 + t
                        turned = pltpu.roll(rows[8 * t : 8 * t + 8], (2 + 4 * m) % 128, 1)
                        packed = jnp.where(quad == m, turned, packed)
            halo_out[group, pl.ds(first // 4 * 8, 8), :] = packed

    for way in range(2):
        for step in range(size):
            h_copy(way, step).start()
    for chunk in range(1, chunks):
        for step in range(1, size):
            a_copy(chunk, step).start()

    band_pad[0:8] = jnp.zeros((8, 9), F32)
    band_pad[8:72] = bands[...]
    band_pad[72:80] = jnp.zeros((8, 9), F32)
    for k in range(9):
        band_rows[k] = jnp.broadcast_to(band_pad[pl.ds(32 * col, 48), k : k + 1], (48, 128))

    @pl.loop(0, cpg)
    def _(c):
        for k in range(9):
            taps[c, k] = wall_w[k, chan0 + c] * band_rows[k]
        for x_group in range(0, xs, 8):
            blank = jnp.zeros((8, 8, 128), F32)
            smooth[c, pl.ds(x_group, 8), pl.ds(pl.multiple_of(40 * col, 8), 8), :] = blank
            gwall[c, pl.ds(x_group, 8), pl.ds(pl.multiple_of(40 * col, 8), 8), :] = blank
        for k in range(9):
            taps_back[c, k] = taps[c, k, pl.ds(12 - k, 32), :]

    red[...] = jnp.zeros((128, 128), F32)

    def shifts(value, edge):
        return (
            pltpu.roll(jnp.where(lane >= 126, edge, value), 2, 1),
            pltpu.roll(jnp.where(lane == 127, edge, value), 1, 1),
            value,
            pltpu.roll(jnp.where(lane == 0, edge, value), 127, 1),
            pltpu.roll(jnp.where(lane < 2, edge, value), 126, 1),
        )

    def filtered(field, c, x, flip):
        total = None
        for i in range(5):
            at = lax.rem(x + (4 - i if flip else i) - 2 + xs, xs)
            for j in range(5):
                term = tile_w[chan0 + c, 5 * i + j] * field[4 - j if flip else j, c, at]
                total = term if total is None else total + term
        return total

    def y_copy(ref, index, send, rec):
        src = pl.multiple_of(32 - 24 * col, 8)
        dst = pl.multiple_of(40 * col, 8)
        return remote(
            ref.at[index + (pl.ds(src, 8),)], ref.at[index + (pl.ds(dst, 8),)],
            send, rec, {"col": other},
        )

    def s_copy(c):
        return y_copy(smooth, (c, pl.ds(0, xs)), s_send.at[c], s_recv.at[c])

    own_copy.wait()
    for way in range(2):
        for step in range(size):
            h_copy(way, step).wait_recv()

    def edges_of(ref_left, ref_right):
        return jnp.where(lax.rem(lane, 4) < 2, ref_left, ref_right)

    for chunk in range(chunks):
        for step in range(1, size):
            a_copy(chunk, step).wait_recv()
        for c in range(chunk * per, chunk * per + per):

            @pl.loop(0, size, unroll=2)
            def _(step, c=c):
                s = source(step)
                stage[step] = recv[step, c].astype(F32)
                at = pl.ds(c // 4 * 8, 8)
                packed = edges_of(halo_in[0, step, at, :], halo_in[1, step, at, :])
                for xl in range(2):
                    rows = stage[step, pl.ds(xl, 32, stride=2), :]
                    for t in range(4):
                        m = c % 4 * 8 + xl * 4 + t
                        edge = pltpu.roll(packed, (126 - 4 * m) % 128, 1)
                        moved = shifts(rows[8 * t : 8 * t + 8], edge)
                        for j in range(5):
                            zfeat[j, c, 2 * s + xl, pl.ds(8 * t, 8), :] = moved[j]

            @pl.loop(0, xs, unroll=4)
            def _(x, c=c):
                smooth[c, x, pl.ds(8, 32), :] = rounded(filtered(zfeat, c, x, False))

            s_copy(c).start()

    for c in range(cpg):
        s_copy(c).wait_recv()

    def p_copy(step):
        return remote(
            part_out.at[step], part_in.at[step], p_send.at[step], p_recv.at[step],
            {"gx": peer(step)},
        )

    def scores_at(x):
        def body(c, totals):
            wall = None
            for k in range(9):
                term = taps[c, k, pl.ds(8, 32), :] * smooth[c, x, pl.ds(4 + k, 32), :]
                wall = term if wall is None else wall + term
            sig = jax.nn.sigmoid(wall)
            hidden = wall * sig
            hid[c, x] = hidden
            slope[c, x] = sig * (1.0 + wall * (1.0 - sig))
            return tuple(
                total + class_w[k, chan0 + c] * hidden for k, total in enumerate(totals)
            )

        return lax.fori_loop(
            0, cpg, body, tuple(jnp.zeros((32, 128), F32) for k in range(4)), unroll=min(4, cpg)
        )

    @pl.loop(1, size)
    def _(step):
        for xl in range(2):
            totals = scores_at(2 * peer(step) + xl)
            for k in range(4):
                part_out[step, pl.ds((2 * k + xl) * 32, 32), :] = totals[k].astype(BF16)
        p_copy(step).start()

    for xl in range(2):
        totals = scores_at(2 * gx + xl)
        for k in range(4):
            part_own[pl.ds((2 * k + xl) * 32, 32), :] = totals[k]

    @pl.loop(1, size)
    def _(step):
        p_copy(step).wait_recv()
        part_own[...] = part_own[...] + part_in[step].astype(F32)

    for xl in range(2):
        marks = labels[pl.ds(64 * col + xl, 32, stride=2), :]
        for k in range(4):
            at = pl.ds((2 * k + xl) * 32, 32)
            err[0, at, :] = (part_own[at, :] - jnp.where(marks == k, 1.0, 0.0)).astype(BF16)

    def e_copy(step):
        return remote(
            err.at[0], err.at[step], e_send.at[step], e_recv.at[step], {"gx": peer(step)}
        )

    for step in range(1, size):
        e_copy(step).start()

    def w_copy(step):
        return y_copy(
            gwall, (pl.ds(0, cpg), pl.ds(2 * source(step), 2)), w_send.at[step], w_recv.at[step]
        )

    def errors_at(step, xl):
        return [err[step, pl.ds((2 * k + xl) * 32, 32), :].astype(F32) for k in range(4)]

    def wall_grads(step):
        for xl in range(2):
            x = 2 * source(step) + xl
            errors = errors_at(step, xl)

            @pl.loop(0, cpg, unroll=min(4, cpg))
            def _(c):
                grad = None
                for k in range(4):
                    term = class_w[k, chan0 + c] * errors[k]
                    grad = term if grad is None else grad + term
                gwall[c, x, pl.ds(8, 32), :] = rounded(grad * slope[c, x])

        w_copy(step).start()

    wall_grads(0)

    @pl.loop(1, size)
    def _(step):
        e_copy(step).wait_recv()
        wall_grads(step)

    @pl.loop(0, size)
    def _(step):
        w_copy(step).wait_recv()

    def g_copy(way, c):
        return remote(
            ghalo_out.at[c], ghalo_in.at[way, c], g_send.at[way, c], g_recv.at[way, c],
            {"gz": right if way == 0 else left},
        )

    @pl.loop(0, cpg)
    def _(c):
        @pl.loop(0, xs, unroll=2)
        def _(x):
            total = None
            for k in range(9):
                term = taps_back[c, k] * gwall[c, x, pl.ds(12 - k, 32), :]
                total = term if total is None else total + term
            gsm[c, x] = rounded(total)

        @pl.loop(0, xgroups)
        def _(group):
            packed = jnp.zeros((8, 128), F32)
            for m in range(32):
                piece = gsm[c, group * 8 + m // 4, pl.ds(m % 4 * 8, 8), :]
                packed = jnp.where(quad == m, pltpu.roll(piece, (2 + 4 * m) % 128, 1), packed)
            ghalo_out[c, group] = packed

        for way in range(2):
            g_copy(way, c).start()

    def o_copy(chunk, step):
        return remote(
            gout.at[peer(step), pl.ds(chunk * per, per)],
            out.at[pl.ds(chan0 + chunk * per, per)],
            o_send.at[chunk, step], o_recv.at[chunk, step], {"gx": peer(step)},
        )

    @pl.loop(0, chunks)
    def _(chunk):
        @pl.loop(0, per)
        def _(lower):
            c = chunk * per + lower
            for way in range(2):
                g_copy(way, c).wait_recv()

            @pl.loop(0, xgroups)
            def _(group):
                packed = edges_of(ghalo_in[0, c, group], ghalo_in[1, c, group])
                for m in range(32):
                    at = pl.ds(m % 4 * 8, 8)
                    x = group * 8 + m // 4
                    edge = pltpu.roll(packed, (126 - 4 * m) % 128, 1)
                    moved = shifts(gsm[c, x, at, :], edge)
                    for j in range(5):
                        zgrad[j, c, x, at, :] = moved[j]

            @pl.loop(0, size, unroll=2)
            def _(s):
                for xl in range(2):
                    gstage[s, pl.ds(xl, 32, stride=2), :] = filtered(zgrad, c, 2 * s + xl, True)
                gout[s, c] = gstage[s].astype(BF16)

            out[chan0 + c] = gout[gx, c]

        for step in range(1, size):
            o_copy(chunk, step).start()

    row = lax.broadcasted_iota(jnp.int32, (8, 128), 0)

    @pl.loop(0, cpg)
    def _(c):
        def body(x, sums25):
            grad = gsm[c, x]
            news = []
            for i in range(5):
                at = lax.rem(x + i - 2 + xs, xs)
                for j in range(5):
                    news.append(sums25[5 * i + j] + fold(zfeat[j, c, at] * grad))
            return tuple(news)

        sums25 = lax.fori_loop(0, xs, body, tuple(jnp.zeros((8, 128), F32) for q in range(25)), unroll=2)

        def wall_body(x, sums9):
            grad = gwall[c, x, pl.ds(8, 32), :]
            news = []
            for k in range(9):
                product = grad * band_rows[k, pl.ds(8, 32), :] * smooth[c, x, pl.ds(4 + k, 32), :]
                news.append(sums9[k] + fold(product))
            return tuple(news)

        def class_body(step, sums4):
            news = list(sums4)
            for xl in range(2):
                hidden = hid[c, 2 * source(step) + xl]
                errors = errors_at(step, xl)
                for k in range(4):
                    news[k] = news[k] + fold(errors[k] * hidden)
            return tuple(news)

        sums9 = lax.fori_loop(
            0, xs, wall_body, tuple(jnp.zeros((8, 128), F32) for k in range(9)), unroll=2
        )
        sums4 = lax.fori_loop(
            0, size, class_body, tuple(jnp.zeros((8, 128), F32) for k in range(4)), unroll=2
        )
        for q, value in enumerate(sums25 + sums9 + sums4):
            red[pl.ds(q, 1), :] = jnp.sum(value, axis=0, keepdims=True)
        line = lax.dot_general(
            jnp.ones((8, 128), F32), red[...], (((1,), (1,)), ((), ())),
            precision=lax.Precision.HIGHEST, preferred_element_type=F32,
        )
        before = jnp.where(c == 0, jnp.zeros((8, 128), F32), sums[me])
        sums[me] = jnp.where(row == c, line, before)

    def r_copy(step):
        return remote(sums.at[me], sums.at[me], r_send.at[step], r_recv.at[step], coords(step))

    @pl.loop(1, everyone)
    def _(step):
        r_copy(step).start()

    @pl.loop(1, everyone)
    def _(step):
        r_copy(step).wait_recv()

    @pl.loop(0, size)
    def _(group):
        total = sums[group * depth * 2]
        for member in range(1, depth * 2):
            total = total + sums[group * depth * 2 + member]
        red[pl.ds(group * cpg, cpg), :] = total[0:cpg] / volume

    turned = red[...].T
    chans = size * cpg
    tile_out[...] = red[0:chans, 0:25]
    wall_out[...] = turned[25:34, 0:chans]
    class_out[...] = turned[34:38, 0:chans]

    for chunk in range(chunks):
        for step in range(1, size):
            o_copy(chunk, step).wait()
            a_copy(chunk, step).wait_send()
    for way in range(2):
        for step in range(size):
            h_copy(way, step).wait_send()
        for c in range(cpg):
            g_copy(way, c).wait_send()
    for c in range(cpg):
        s_copy(c).wait_send()
    for step in range(1, size):
        p_copy(step).wait_send()
        e_copy(step).wait_send()
    for step in range(size):
        w_copy(step).wait_send()

    @pl.loop(1, everyone)
    def _(step):
        r_copy(step).wait_send()


def shards(features, labels, grid_index, stretch, tile_filter, wall_filter, class_weight):
    chans, rows, cells_x, cells_z = features.shape
    size, depth = lax.axis_size("gx"), lax.axis_size("gz")
    volume = labels.shape[0] * cells_x * size * cells_z * depth
    cpg = chans // size
    chunks = min(4, cpg)
    per_dest = max(cpg // 4, 1) * 8
    xs = 2 * size
    everyone = size * depth * 2
    onehot = (grid_index[:, None] == jnp.arange(stretch.shape[0], dtype=jnp.int32)).astype(F32)
    bands = jnp.dot(onehot, stretch, precision=lax.Precision.HIGHEST)
    dma = pltpu.SemaphoreType.DMA
    vmem = pl.BlockSpec(memory_space=pltpu.VMEM)
    smem = pl.BlockSpec(memory_space=pltpu.SMEM)
    grad, tile_grad, wall_grad, class_grad = pl.pallas_call(
        functools.partial(kernel, (size, depth, cpg, chunks, volume)),
        out_shape=(
            jax.ShapeDtypeStruct((chans, 64, 128), BF16),
            jax.ShapeDtypeStruct((chans, 25), F32),
            jax.ShapeDtypeStruct((9, chans), F32),
            jax.ShapeDtypeStruct((4, chans), F32),
        ),
        in_specs=[vmem, vmem, vmem, smem, smem, smem],
        out_specs=(vmem, vmem, vmem, vmem),
        scratch_shapes=[
            pltpu.VMEM((size, cpg, 64, 128), BF16),
            pltpu.VMEM((80, 9), F32),
            pltpu.VMEM((size, per_dest, 128), F32),
            pltpu.VMEM((2, size, per_dest, 128), F32),
            pltpu.VMEM((5, cpg, xs, 32, 128), F32),
            pltpu.VMEM((cpg, xs, 48, 128), F32),
            pltpu.VMEM((max(cpg, size), 64, 128), F32),
            pltpu.VMEM((cpg, 9, 48, 128), F32),
            pltpu.VMEM((9, 48, 128), F32),
            pltpu.VMEM((cpg, xs, 32, 128), F32),
            pltpu.VMEM((cpg, xs, 32, 128), F32),
            pltpu.VMEM((256, 128), F32),
            pltpu.VMEM((size, 256, 128), BF16),
            pltpu.VMEM((size, 256, 128), BF16),
            pltpu.VMEM((size, 256, 128), BF16),
            pltpu.VMEM((cpg, xs, 48, 128), F32),
            pltpu.VMEM((cpg, xs, 32, 128), F32),
            pltpu.VMEM((cpg, xs // 8, 8, 128), F32),
            pltpu.VMEM((2, cpg, xs // 8, 8, 128), F32),
            pltpu.VMEM((5, cpg, xs, 32, 128), F32),
            pltpu.VMEM((size, cpg, 64, 128), BF16),
            pltpu.VMEM((size, 64, 128), F32),
            pltpu.VMEM((cpg, 9, 32, 128), F32),
            pltpu.VMEM((128, 128), F32),
            pltpu.VMEM((everyone, 8, 128), F32),
            dma((chunks, size)), dma((chunks, size)), dma(()),
            dma((2, size)), dma((2, size)),
            dma((cpg,)), dma((cpg,)),
            dma((size,)), dma((size,)),
            dma((size,)), dma((size,)),
            dma((size,)), dma((size,)),
            dma((2, cpg)), dma((2, cpg)),
            dma((chunks, size)), dma((chunks, size)),
            dma((everyone,)), dma((everyone,)),
        ],
        compiler_params=pltpu.CompilerParams(
            collective_id=0, has_side_effects=True, vmem_limit_bytes=48 * 1024 * 1024
        ),
    )(
        features.reshape(chans, 64, 128), labels.reshape(128, 128), bands,
        tile_filter, wall_filter.T, class_weight,
    )
    return grad.reshape(features.shape), tile_grad, wall_grad.T, class_grad


def solution(mesh):
    return jax.shard_map(
        shards,
        mesh=mesh,
        in_specs=(
            P(None, "col", ("group", "gx"), "gz"),
            P(None, ("group", "gx"), "gz"),
            P(),
            P(),
            P(),
            P(),
            P(),
        ),
        out_specs=(
            P(None, "col", ("group", "gx"), "gz"),
            P("group", None),
            P("group", None),
            P("group", None),
        ),
        check_vma=False,
    )
```

```python
import functools

import jax
import jax.numpy as jnp
from jax import lax
from jax.experimental import pallas as pl
from jax.experimental.pallas import tpu as pltpu
from jax.sharding import PartitionSpec as P

F32 = jnp.float32
BF16 = jnp.bfloat16
MESH = pl.DeviceIdType.MESH


def fold(value):
    total = value[0:8]
    for row in range(8, value.shape[0], 8):
        total = total + value[row : row + 8]
    return total


def rounded(value):
    return value.astype(BF16).astype(F32)


def kernel(
    dims,
    feat, labels, bands, tile_w, wall_w, class_w,
    out, tile_out, wall_out, class_out,
    recv, band_pad, halo_out, halo_in, zfeat, smooth, stage, taps, band_rows, hid, slope,
    part_own, part_out, part_in, err, gwall, gsm, ghalo_out, ghalo_in, zgrad, gout, gstage,
    taps_back, acc, red, sums,
    a_send, a_recv, own_sem, h_send, h_recv, s_send, s_recv, p_send, p_recv, e_send, e_recv,
    w_send, w_recv, g_send, g_recv, o_send, o_recv, r_send, r_recv,
):
    size, depth, cpg, chunks, volume = dims
    per = cpg // chunks
    xs = 2 * size
    xgroups = xs // 8
    everyone = size * depth * 2
    gx, gz, col = lax.axis_index("gx"), lax.axis_index("gz"), lax.axis_index("col")
    me = (gx * depth + gz) * 2 + col
    other = 1 - col
    right, left = lax.rem(gz + 1, depth), lax.rem(gz + depth - 1, depth)
    chan0 = gx * cpg

    def peer(step):
        return lax.rem(gx + step, size)

    def source(step):
        return lax.rem(gx + size - step, size)

    def coords(step):
        index = lax.rem(me + step, everyone)
        return {
            "gx": index // (2 * depth),
            "gz": lax.rem(index // 2, depth),
            "col": lax.rem(index, 2),
        }

    barrier = pltpu.get_barrier_semaphore()

    @pl.loop(1, everyone)
    def _(step):
        pl.semaphore_signal(barrier, inc=1, device_id=coords(step), device_id_type=MESH)

    pl.semaphore_wait(barrier, everyone - 1)

    def remote(src, dst, send, rec, device):
        return pltpu.make_async_remote_copy(
            src_ref=src, dst_ref=dst, send_sem=send, recv_sem=rec,
            device_id=device, device_id_type=MESH,
        )

    def a_copy(chunk, step):
        return remote(
            feat.at[pl.ds(peer(step) * cpg + chunk * per, per)],
            recv.at[step, pl.ds(chunk * per, per)],
            a_send.at[chunk, step], a_recv.at[chunk, step], {"gx": peer(step)},
        )

    def h_copy(way, step):
        return remote(
            halo_out.at[peer(step)], halo_in.at[way, step],
            h_send.at[way, step], h_recv.at[way, step],
            {"gx": peer(step), "gz": right if way == 0 else left},
        )

    own_copy = pltpu.make_async_copy(feat.at[pl.ds(chan0, cpg)], recv.at[0], own_sem)
    own_copy.start()
    for step in range(1, size):
        a_copy(0, step).start()

    lane = lax.broadcasted_iota(jnp.int32, (8, 128), 1)
    quad = lane // 4

    @pl.loop(0, size)
    def _(group):
        for first in range(0, cpg, 4):
            packed = jnp.zeros((8, 128), F32)
            for c in range(first, min(first + 4, cpg)):
                stage[c] = feat[group * cpg + c].astype(F32)
                for xl in range(2):
                    rows = stage[c, pl.ds(xl, 32, stride=2), :]
                    for t in range(4):
                        m = (c - first) * 8 + xl * 4 + t
                        turned = pltpu.roll(rows[8 * t : 8 * t + 8], (2 + 4 * m) % 128, 1)
                        packed = jnp.where(quad == m, turned, packed)
            halo_out[group, pl.ds(first // 4 * 8, 8), :] = packed

    for way in range(2):
        for step in range(size):
            h_copy(way, step).start()
    for chunk in range(1, chunks):
        for step in range(1, size):
            a_copy(chunk, step).start()

    band_pad[0:8] = jnp.zeros((8, 9), F32)
    band_pad[8:72] = bands[...]
    band_pad[72:80] = jnp.zeros((8, 9), F32)
    for k in range(9):
        band_rows[k] = jnp.broadcast_to(band_pad[pl.ds(32 * col, 48), k : k + 1], (48, 128))

    @pl.loop(0, cpg)
    def _(c):
        for k in range(9):
            taps[c, k] = wall_w[k, chan0 + c] * band_rows[k]
        for x_group in range(0, xs, 8):
            blank = jnp.zeros((8, 8, 128), F32)
            smooth[c, pl.ds(x_group, 8), pl.ds(pl.multiple_of(40 * col, 8), 8), :] = blank
            gwall[c, pl.ds(x_group, 8), pl.ds(pl.multiple_of(40 * col, 8), 8), :] = blank
        for k in range(9):
            taps_back[c, k] = taps[c, k, pl.ds(12 - k, 32), :]

    red[...] = jnp.zeros((128, 128), F32)

    def shifts(value, edge):
        return (
            pltpu.roll(jnp.where(lane >= 126, edge, value), 2, 1),
            pltpu.roll(jnp.where(lane == 127, edge, value), 1, 1),
            value,
            pltpu.roll(jnp.where(lane == 0, edge, value), 127, 1),
            pltpu.roll(jnp.where(lane < 2, edge, value), 126, 1),
        )

    def filtered(field, c, x, flip):
        total = None
        for i in range(5):
            at = lax.rem(x + (4 - i if flip else i) - 2 + xs, xs)
            for j in range(5):
                term = tile_w[chan0 + c, 5 * i + j] * field[4 - j if flip else j, c, at]
                total = term if total is None else total + term
        return total

    def y_copy(ref, index, send, rec):
        src = pl.multiple_of(32 - 24 * col, 8)
        dst = pl.multiple_of(40 * col, 8)
        return remote(
            ref.at[index + (pl.ds(src, 8),)], ref.at[index + (pl.ds(dst, 8),)],
            send, rec, {"col": other},
        )

    def s_copy(c):
        return y_copy(smooth, (c, pl.ds(0, xs)), s_send.at[c], s_recv.at[c])

    own_copy.wait()
    for way in range(2):
        for step in range(size):
            h_copy(way, step).wait_recv()

    def edges_of(ref_left, ref_right):
        return jnp.where(lax.rem(lane, 4) < 2, ref_left, ref_right)

    for chunk in range(chunks):
        for step in range(1, size):
            a_copy(chunk, step).wait_recv()
        for c in range(chunk * per, chunk * per + per):

            @pl.loop(0, size, unroll=2)
            def _(step, c=c):
                s = source(step)
                stage[step] = recv[step, c].astype(F32)
                at = pl.ds(c // 4 * 8, 8)
                packed = edges_of(halo_in[0, step, at, :], halo_in[1, step, at, :])
                for xl in range(2):
                    rows = stage[step, pl.ds(xl, 32, stride=2), :]
                    for t in range(4):
                        m = c % 4 * 8 + xl * 4 + t
                        edge = pltpu.roll(packed, (126 - 4 * m) % 128, 1)
                        moved = shifts(rows[8 * t : 8 * t + 8], edge)
                        for j in range(5):
                            zfeat[j, c, 2 * s + xl, pl.ds(8 * t, 8), :] = moved[j]

            @pl.loop(0, xs, unroll=4)
            def _(x, c=c):
                smooth[c, x, pl.ds(8, 32), :] = rounded(filtered(zfeat, c, x, False))

            s_copy(c).start()

    for c in range(cpg):
        s_copy(c).wait_recv()

    def p_copy(step):
        return remote(
            part_out.at[step], part_in.at[step], p_send.at[step], p_recv.at[step],
            {"gx": peer(step)},
        )

    def scores_at(x):
        def body(c, totals):
            wall = None
            for k in range(9):
                term = taps[c, k, pl.ds(8, 32), :] * smooth[c, x, pl.ds(4 + k, 32), :]
                wall = term if wall is None else wall + term
            sig = jax.nn.sigmoid(wall)
            hidden = wall * sig
            hid[c, x] = hidden
            slope[c, x] = sig * (1.0 + wall * (1.0 - sig))
            return tuple(
                total + class_w[k, chan0 + c] * hidden for k, total in enumerate(totals)
            )

        return lax.fori_loop(
            0, cpg, body, tuple(jnp.zeros((32, 128), F32) for k in range(4)), unroll=min(4, cpg)
        )

    @pl.loop(1, size)
    def _(step):
        for xl in range(2):
            totals = scores_at(2 * peer(step) + xl)
            for k in range(4):
                part_out[step, pl.ds((2 * k + xl) * 32, 32), :] = totals[k].astype(BF16)
        p_copy(step).start()

    for xl in range(2):
        totals = scores_at(2 * gx + xl)
        for k in range(4):
            part_own[pl.ds((2 * k + xl) * 32, 32), :] = totals[k]

    @pl.loop(1, size)
    def _(step):
        p_copy(step).wait_recv()
        part_own[...] = part_own[...] + part_in[step].astype(F32)

    for xl in range(2):
        marks = labels[pl.ds(64 * col + xl, 32, stride=2), :]
        for k in range(4):
            at = pl.ds((2 * k + xl) * 32, 32)
            err[0, at, :] = (part_own[at, :] - jnp.where(marks == k, 1.0, 0.0)).astype(BF16)

    def e_copy(step):
        return remote(
            err.at[0], err.at[step], e_send.at[step], e_recv.at[step], {"gx": peer(step)}
        )

    for step in range(1, size):
        e_copy(step).start()

    def w_copy(step):
        return y_copy(
            gwall, (pl.ds(0, cpg), pl.ds(2 * source(step), 2)), w_send.at[step], w_recv.at[step]
        )

    def errors_at(step, xl):
        return [err[step, pl.ds((2 * k + xl) * 32, 32), :].astype(F32) for k in range(4)]

    def wall_grads(step):
        for xl in range(2):
            x = 2 * source(step) + xl
            errors = errors_at(step, xl)

            @pl.loop(0, cpg, unroll=min(4, cpg))
            def _(c):
                grad = None
                for k in range(4):
                    term = class_w[k, chan0 + c] * errors[k]
                    grad = term if grad is None else grad + term
                gwall[c, x, pl.ds(8, 32), :] = rounded(grad * slope[c, x])

        w_copy(step).start()

    wall_grads(0)

    @pl.loop(1, size)
    def _(step):
        e_copy(step).wait_recv()
        wall_grads(step)

    @pl.loop(0, cpg)
    def _(c):
        def wall_body(x, sums9):
            grad = gwall[c, x, pl.ds(8, 32), :]
            news = []
            for k in range(9):
                product = grad * band_rows[k, pl.ds(8, 32), :] * smooth[c, x, pl.ds(4 + k, 32), :]
                news.append(sums9[k] + fold(product))
            return tuple(news)

        def class_body(step, sums4):
            news = list(sums4)
            for xl in range(2):
                hidden = hid[c, 2 * source(step) + xl]
                errors = errors_at(step, xl)
                for k in range(4):
                    news[k] = news[k] + fold(errors[k] * hidden)
            return tuple(news)

        sums9 = lax.fori_loop(
            0, xs, wall_body, tuple(jnp.zeros((8, 128), F32) for k in range(9)), unroll=2
        )
        sums4 = lax.fori_loop(
            0, size, class_body, tuple(jnp.zeros((8, 128), F32) for k in range(4)), unroll=2
        )
        for q, value in enumerate(sums9 + sums4):
            acc[c, q] = value

    @pl.loop(0, size)
    def _(step):
        w_copy(step).wait_recv()

    def g_copy(way, c):
        return remote(
            ghalo_out.at[c], ghalo_in.at[way, c], g_send.at[way, c], g_recv.at[way, c],
            {"gz": right if way == 0 else left},
        )

    @pl.loop(0, cpg)
    def _(c):
        @pl.loop(0, xs, unroll=2)
        def _(x):
            total = None
            for k in range(9):
                term = taps_back[c, k] * gwall[c, x, pl.ds(12 - k, 32), :]
                total = term if total is None else total + term
            gsm[c, x] = rounded(total)

        @pl.loop(0, xgroups)
        def _(group):
            packed = jnp.zeros((8, 128), F32)
            for m in range(32):
                piece = gsm[c, group * 8 + m // 4, pl.ds(m % 4 * 8, 8), :]
                packed = jnp.where(quad == m, pltpu.roll(piece, (2 + 4 * m) % 128, 1), packed)
            ghalo_out[c, group] = packed

        for way in range(2):
            g_copy(way, c).start()

    def o_copy(chunk, step):
        return remote(
            gout.at[peer(step), pl.ds(chunk * per, per)],
            out.at[pl.ds(chan0 + chunk * per, per)],
            o_send.at[chunk, step], o_recv.at[chunk, step], {"gx": peer(step)},
        )

    @pl.loop(0, chunks)
    def _(chunk):
        @pl.loop(0, per)
        def _(lower):
            c = chunk * per + lower
            for way in range(2):
                g_copy(way, c).wait_recv()

            @pl.loop(0, xgroups)
            def _(group):
                packed = edges_of(ghalo_in[0, c, group], ghalo_in[1, c, group])
                for m in range(32):
                    at = pl.ds(m % 4 * 8, 8)
                    x = group * 8 + m // 4
                    edge = pltpu.roll(packed, (126 - 4 * m) % 128, 1)
                    moved = shifts(gsm[c, x, at, :], edge)
                    for j in range(5):
                        zgrad[j, c, x, at, :] = moved[j]

            @pl.loop(0, size, unroll=2)
            def _(s):
                for xl in range(2):
                    gstage[s, pl.ds(xl, 32, stride=2), :] = filtered(zgrad, c, 2 * s + xl, True)
                gout[s, c] = gstage[s].astype(BF16)

            out[chan0 + c] = gout[gx, c]

        for step in range(1, size):
            o_copy(chunk, step).start()

    row = lax.broadcasted_iota(jnp.int32, (8, 128), 0)

    @pl.loop(0, cpg)
    def _(c):
        def body(x, sums25):
            grad = gsm[c, x]
            news = []
            for i in range(5):
                at = lax.rem(x + i - 2 + xs, xs)
                for j in range(5):
                    news.append(sums25[5 * i + j] + fold(zfeat[j, c, at] * grad))
            return tuple(news)

        sums25 = lax.fori_loop(0, xs, body, tuple(jnp.zeros((8, 128), F32) for q in range(25)), unroll=2)
        for q in range(38):
            value = sums25[q] if q < 25 else acc[c, q - 25]
            red[pl.ds(q, 1), :] = jnp.sum(value, axis=0, keepdims=True)
        line = lax.dot_general(
            jnp.ones((8, 128), F32), red[...], (((1,), (1,)), ((), ())),
            precision=lax.Precision.HIGHEST, preferred_element_type=F32,
        )
        before = jnp.where(c == 0, jnp.zeros((8, 128), F32), sums[me])
        sums[me] = jnp.where(row == c, line, before)

    def r_copy(step):
        return remote(sums.at[me], sums.at[me], r_send.at[step], r_recv.at[step], coords(step))

    @pl.loop(1, everyone)
    def _(step):
        r_copy(step).start()

    @pl.loop(1, everyone)
    def _(step):
        r_copy(step).wait_recv()

    @pl.loop(0, size)
    def _(group):
        total = sums[group * depth * 2]
        for member in range(1, depth * 2):
            total = total + sums[group * depth * 2 + member]
        red[pl.ds(group * cpg, cpg), :] = total[0:cpg] / volume

    turned = red[...].T
    chans = size * cpg
    tile_out[...] = red[0:chans, 0:25]
    wall_out[...] = turned[25:34, 0:chans]
    class_out[...] = turned[34:38, 0:chans]

    for chunk in range(chunks):
        for step in range(1, size):
            o_copy(chunk, step).wait()
            a_copy(chunk, step).wait_send()
    for way in range(2):
        for step in range(size):
            h_copy(way, step).wait_send()
        for c in range(cpg):
            g_copy(way, c).wait_send()
    for c in range(cpg):
        s_copy(c).wait_send()
    for step in range(1, size):
        p_copy(step).wait_send()
        e_copy(step).wait_send()
    for step in range(size):
        w_copy(step).wait_send()

    @pl.loop(1, everyone)
    def _(step):
        r_copy(step).wait_send()


def shards(features, labels, grid_index, stretch, tile_filter, wall_filter, class_weight):
    chans, rows, cells_x, cells_z = features.shape
    size, depth = lax.axis_size("gx"), lax.axis_size("gz")
    volume = labels.shape[0] * cells_x * size * cells_z * depth
    cpg = chans // size
    chunks = min(4, cpg)
    per_dest = max(cpg // 4, 1) * 8
    xs = 2 * size
    everyone = size * depth * 2
    onehot = (grid_index[:, None] == jnp.arange(stretch.shape[0], dtype=jnp.int32)).astype(F32)
    bands = jnp.dot(onehot, stretch, precision=lax.Precision.HIGHEST)
    dma = pltpu.SemaphoreType.DMA
    vmem = pl.BlockSpec(memory_space=pltpu.VMEM)
    smem = pl.BlockSpec(memory_space=pltpu.SMEM)
    grad, tile_grad, wall_grad, class_grad = pl.pallas_call(
        functools.partial(kernel, (size, depth, cpg, chunks, volume)),
        out_shape=(
            jax.ShapeDtypeStruct((chans, 64, 128), BF16),
            jax.ShapeDtypeStruct((chans, 25), F32),
            jax.ShapeDtypeStruct((9, chans), F32),
            jax.ShapeDtypeStruct((4, chans), F32),
        ),
        in_specs=[vmem, vmem, vmem, smem, smem, smem],
        out_specs=(vmem, vmem, vmem, vmem),
        scratch_shapes=[
            pltpu.VMEM((size, cpg, 64, 128), BF16),
            pltpu.VMEM((80, 9), F32),
            pltpu.VMEM((size, per_dest, 128), F32),
            pltpu.VMEM((2, size, per_dest, 128), F32),
            pltpu.VMEM((5, cpg, xs, 32, 128), F32),
            pltpu.VMEM((cpg, xs, 48, 128), F32),
            pltpu.VMEM((max(cpg, size), 64, 128), F32),
            pltpu.VMEM((cpg, 9, 48, 128), F32),
            pltpu.VMEM((9, 48, 128), F32),
            pltpu.VMEM((cpg, xs, 32, 128), F32),
            pltpu.VMEM((cpg, xs, 32, 128), F32),
            pltpu.VMEM((256, 128), F32),
            pltpu.VMEM((size, 256, 128), BF16),
            pltpu.VMEM((size, 256, 128), BF16),
            pltpu.VMEM((size, 256, 128), BF16),
            pltpu.VMEM((cpg, xs, 48, 128), F32),
            pltpu.VMEM((cpg, xs, 32, 128), F32),
            pltpu.VMEM((cpg, xs // 8, 8, 128), F32),
            pltpu.VMEM((2, cpg, xs // 8, 8, 128), F32),
            pltpu.VMEM((5, cpg, xs, 32, 128), F32),
            pltpu.VMEM((size, cpg, 64, 128), BF16),
            pltpu.VMEM((size, 64, 128), F32),
            pltpu.VMEM((cpg, 9, 32, 128), F32),
            pltpu.VMEM((cpg, 13, 8, 128), F32),
            pltpu.VMEM((128, 128), F32),
            pltpu.VMEM((everyone, 8, 128), F32),
            dma((chunks, size)), dma((chunks, size)), dma(()),
            dma((2, size)), dma((2, size)),
            dma((cpg,)), dma((cpg,)),
            dma((size,)), dma((size,)),
            dma((size,)), dma((size,)),
            dma((size,)), dma((size,)),
            dma((2, cpg)), dma((2, cpg)),
            dma((chunks, size)), dma((chunks, size)),
            dma((everyone,)), dma((everyone,)),
        ],
        compiler_params=pltpu.CompilerParams(
            collective_id=0, has_side_effects=True, vmem_limit_bytes=48 * 1024 * 1024
        ),
    )(
        features.reshape(chans, 64, 128), labels.reshape(128, 128), bands,
        tile_filter, wall_filter.T, class_weight,
    )
    return grad.reshape(features.shape), tile_grad, wall_grad.T, class_grad


def solution(mesh):
    return jax.shard_map(
        shards,
        mesh=mesh,
        in_specs=(
            P(None, "col", ("group", "gx"), "gz"),
            P(None, ("group", "gx"), "gz"),
            P(),
            P(),
            P(),
            P(),
            P(),
        ),
        out_specs=(
            P(None, "col", ("group", "gx"), "gz"),
            P("group", None),
            P("group", None),
            P("group", None),
        ),
        check_vma=False,
    )
```
